32 devices in a mesh: row: 8 (over z, core), col: 4 (over y, x).
Axes of the slice: x: 2, y: 2, z: 4, core: 2. Of those that a mesh axis runs over, the one named last changes fastest.
Arguments:
- snapshots: float32 [12288, 2048], P('row', 'col'), may hold values from -6 to 6
- mass: float32 [12288], P('row'), may hold values from 1 to 30, as said below
Outputs:
- gram: float32 [2048, 2048], P('col', 'row')
The draws below stay inside these ranges and needn't reach their ends.
Inputs may be any that keep to these rules, and one draw needn't show every extreme that they name: `mass`: positive lumped masses.
All inputs are finite; a program needn't handle non-finite values.
Results may differ from the reference program's by a relative error of at most 0.00005.
Values sent between devices are 32-bit elements; how exact they have to be, the bound alone decides.
A program may use at most 128 MiB of HBM per device.

```python
import jax
import jax.numpy as jnp
from jax import lax

ROWS = 12288
NCOL = 2048


def draw_mass(key, part):
    key = jax.random.fold_in(key, 7)
    ramp = jnp.arange(ROWS, dtype=jnp.float32) / ROWS
    unit = jax.random.uniform(key, (ROWS,), jnp.float32)
    factor = jnp.exp(unit * jnp.log(10.0))
    return jnp.exp(ramp * jnp.log(3.0)) * factor


def with_spikes(result, rng, source, target, shards_of, factor):
    def block_of(position):
        return (jnp.arange(result.shape[position]) // (result.shape[position] // shards_of)).reshape((-1,) + (1,) * (result.ndim - 1 - position))

    first = jax.random.permutation(rng, shards_of)[block_of(target)]
    second = (block_of(target) + shards_of // 2) % shards_of
    return jnp.where((block_of(source) == first) | (block_of(source) == second), factor * result, result)


def steps_of(rng, shape, split, smallest, largest):
    level, own = 1.0, jax.random.fold_in(rng, 6)
    for dim, blocks in split:
        steps = jnp.exp(jax.random.uniform(jax.random.fold_in(own, dim), (blocks,), jnp.float32, smallest / len(split), largest / len(split)))
        level = level * jnp.repeat(steps, shape[dim] // blocks).reshape([-1 if axis == dim else 1 for axis in range(len(shape))])
    return level


def bell_draw_with(own_key, shape, scale, limit, pieces, heavy, kind=jnp.bfloat16):
    drawn = scale * jax.random.normal(own_key, shape, jnp.float32)
    if pieces:
        drawn = drawn * steps_of(own_key, shape, pieces, -0.22, 0.18)
    return jnp.clip(with_spikes(drawn, jax.random.fold_in(own_key, 3), *heavy), -limit, limit).astype(kind)


def setup_inputs(seed: int = 0) -> dict:
    key_list = jax.random.split(jax.random.key(seed), 3)
    snapshots = bell_draw_with(key_list[0], (ROWS, NCOL), 1.0, 6.0, ((0, 8), (1, 4)), (0, 1, 8, 2.0), jnp.float32)
    mass = draw_mass(jax.random.fold_in(key_list[2], 71), 0)
    return dict(snapshots=snapshots, mass=mass)


def contract(left, right):
    return lax.dot_general(left, right, (((0,), (0,)), ((), ())), precision=lax.Precision.HIGHEST, preferred_element_type=jnp.float32)


def reference(snapshots, mass):
    total = jnp.sum(mass)
    weighted = snapshots * mass[:, None]
    return contract(weighted, snapshots) / total
```

```python
import functools

import jax
import jax.numpy as jnp
from jax import lax
from jax.experimental import pallas as pl
from jax.experimental.pallas import tpu as pltpu
from jax.sharding import PartitionSpec as P

MESH = pl.DeviceIdType.MESH
LANES = 128
EXTRA = 8


def halves(value):
    high = value.astype(jnp.bfloat16)
    low = (value - high.astype(jnp.float32)).astype(jnp.bfloat16)
    return high, low


def product(left_high, left_low, right_high, right_low):
    dot = functools.partial(jnp.dot, preferred_element_type=jnp.float32)
    return dot(left_high, right_high) + (dot(left_high, right_low) + dot(left_low, right_high))


def kernel(
    rows_n, cols_n, s_ref, mass_ref, out_ref,
    rhs, lhs_high, lhs_low, kept, given, taken, swapped, landed,
    y_send, y_recv, own_send, fwd_send, x_recv,
    core_send, core_recv, swap_send, swap_recv, z_send, z_recv,
):
    row, col = lax.axis_index("row"), lax.axis_index("col")
    lo_n, z_n = cols_n // 2, rows_n // 2
    core, z = lax.rem(row, 2), row // 2
    hi, lo = col // lo_n, lax.rem(col, lo_n)
    depth, block = s_ref.shape[0] // 2, s_ref.shape[1]
    slices = block // LANES
    width = out_ref.shape[1]
    subs = width // LANES
    per_block = block // (2 * LANES)
    units = per_block * cols_n
    z_per_block = per_block // subs

    sibling = (row + 1 - 2 * core, col)
    across = (row, (1 - hi) * lo_n + lo)

    def along(d):
        return (row, hi * lo_n + lax.rem(lo + lo_n - d, lo_n))

    def layer(other):
        return (other * 2 + core, col)

    def part(half, sl):
        return s_ref.at[pl.ds(pl.multiple_of(half * depth, depth), depth), pl.ds(sl * LANES, LANES)]

    def copy(src, dst, send, recv, device):
        return pltpu.make_async_remote_copy(
            src_ref=src, dst_ref=dst, send_sem=send, recv_sem=recv, device_id=device, device_id_type=MESH
        )

    def y_copy(sl):
        return copy(part(1 - hi, sl), rhs.at[hi, sl], y_send.at[sl], y_recv.at[sl], across)

    def own_copy(d, sl):
        at = 2 * d + hi
        return copy(part(hi, sl), rhs.at[at, sl], own_send.at[d, sl], x_recv.at[at, sl], along(d))

    def fwd_copy(d, sl):
        at = 2 * d + 1 - hi
        return copy(rhs.at[1 - hi, sl], rhs.at[at, sl], fwd_send.at[d, sl], x_recv.at[at, sl], along(d))

    def core_copy(u):
        return copy(given.at[u], taken.at[u], core_send.at[u], core_recv.at[u], sibling)

    def swap_copy(u):
        return copy(kept.at[u, 1], swapped.at[u], swap_send.at[u], swap_recv.at[u], across)

    def place(u):
        t, rest = u // cols_n, lax.rem(u, cols_n)
        d, e = rest // 2, lax.rem(rest, 2)
        which = lax.rem(e + z, 2)
        at = 2 * d + which
        col_block = which * lo_n + lax.rem(lo + d, lo_n)
        target = col_block * z_per_block + t // subs
        return t, d, at, target, lax.rem(t, subs)

    def slice_of(k, t):
        return (2 * (t // subs) + k) * subs + lax.rem(t, subs)

    def z_copy(u):
        _, _, _, target, sub = place(u)
        return copy(kept.at[u, 0], landed.at[z, sub], z_send.at[u], z_recv.at[z, sub], layer(target))

    peers = [sibling, across] + [along(d) for d in range(1, lo_n)]
    peers += [layer(lax.rem(z + d, z_n)) for d in range(1, z_n)]
    barrier = pltpu.get_barrier_semaphore()
    for peer in peers:
        pl.semaphore_signal(barrier, inc=1, device_id=peer, device_id_type=MESH)
    pl.semaphore_wait(barrier, len(peers))

    for sl in range(slices):
        y_copy(sl).start()
        for d in range(1, lo_n):
            own_copy(d, sl).start()

    mass = mass_ref[pl.ds(pl.multiple_of(hi * depth, depth), depth), :]
    summed = jnp.broadcast_to(jnp.sum(mass, axis=0, keepdims=True), (EXTRA, LANES))

    def put_left(first, sl, value):
        high, low = halves(jnp.transpose(value * mass))
        at = pl.ds(first + sl * LANES, LANES)
        lhs_high[at, :] = high
        lhs_low[at, :] = low

    for sl in range(slices):
        value = part(hi, sl)[...]
        rhs[hi, sl] = value
        put_left(0, sl, value)
    for sl in range(slices):
        y_copy(sl).wait_recv()
        for d in range(1, lo_n):
            fwd_copy(d, sl).start()
        put_left(block, sl, rhs[1 - hi, sl])

    def compute(u):
        t, d, at, _, _ = place(u)
        mine, theirs = slice_of(core, t), slice_of(1 - core, t)

        @pl.when(d > 0)
        def _():
            for sl in (mine, theirs):
                copy(rhs.at[at, sl], rhs.at[at, sl], own_send.at[0, 0], x_recv.at[at, sl], along(1)).wait_recv()

        right = jnp.concatenate([rhs[at, mine], rhs[at, theirs]], axis=1)
        high, low = halves(right)
        for side in range(2):
            at_rows = pl.ds(side * block, block)
            value = product(lhs_high[at_rows, :], lhs_low[at_rows, :], high, low)
            kept[u, side, :block, :] = value[:, :LANES]
            given[u, side, :block, :] = value[:, LANES:]
            kept[u, side, block:, :] = summed
            given[u, side, block:, :] = summed
        core_copy(u).start()

    def join_cores(u):
        core_copy(u).wait_recv()
        kept[u, 1] = kept[u, 1] + taken[u, 1]
        swap_copy(u).start()
        kept[u, 0] = kept[u, 0] + taken[u, 0]

    def join_across(u):
        _, _, _, target, sub = place(u)
        swap_copy(u).wait_recv()
        value = kept[u, 0] + swapped[u]

        @pl.when(target == z)
        def _():
            landed[z, sub] = value

        @pl.when(target != z)
        def _():
            kept[u, 0] = value
            z_copy(u).start()

    def step(i, carry):
        @pl.when(i < units)
        def _():
            compute(i)

        @pl.when((i >= 1) & (i < units + 1))
        def _():
            join_cores(i - 1)

        @pl.when(i >= 2)
        def _():
            join_across(i - 2)

        return carry

    lax.fori_loop(0, units + 2, step, 0)

    for d in range(1, z_n):
        source = lax.rem(z + d, z_n)
        for sub in range(subs):
            copy(
                landed.at[source, sub], landed.at[source, sub], z_send.at[0], z_recv.at[source, sub], layer(source)
            ).wait_recv()
    for sub in range(subs):
        value = landed[0, sub]
        for source in range(1, z_n):
            value = value + landed[source, sub]
        out_ref[:, sub * LANES : (sub + 1) * LANES] = value[:block] / value[block : block + 1]

    for sl in range(slices):
        y_copy(sl).wait_send()
        for d in range(1, lo_n):
            own_copy(d, sl).wait_send()
            fwd_copy(d, sl).wait_send()

    def drain(u, carry):
        core_copy(u).wait_send()
        swap_copy(u).wait_send()

        @pl.when(place(u)[3] != z)
        def _():
            z_copy(u).wait_send()

        return carry

    lax.fori_loop(0, units, drain, 0)


def solution(mesh):
    rows_n, cols_n = mesh.shape["row"], mesh.shape["col"]

    def shards(snapshots, mass):
        rows, block = snapshots.shape
        depth, slices, lo_n, z_n = rows // 2, block // LANES, cols_n // 2, rows_n // 2
        width = block * cols_n // rows_n
        subs = width // LANES
        units = block // (2 * LANES) * cols_n
        piece = (block + EXTRA, LANES)
        dma = pltpu.SemaphoreType.DMA
        flops = 2 * depth * 2 * block * block * cols_n * 3
        return pl.pallas_call(
            functools.partial(kernel, rows_n, cols_n),
            out_shape=jax.ShapeDtypeStruct((block, width), jnp.float32),
            in_specs=[pl.BlockSpec(memory_space=pltpu.VMEM)] * 2,
            out_specs=pl.BlockSpec(memory_space=pltpu.VMEM),
            scratch_shapes=[
                pltpu.VMEM((cols_n, slices, depth, LANES), jnp.float32),
                pltpu.VMEM((2 * block, depth), jnp.bfloat16),
                pltpu.VMEM((2 * block, depth), jnp.bfloat16),
                pltpu.VMEM((units, 2) + piece, jnp.float32),
                pltpu.VMEM((units, 2) + piece, jnp.float32),
                pltpu.VMEM((units, 2) + piece, jnp.float32),
                pltpu.VMEM((units,) + piece, jnp.float32),
                pltpu.VMEM((z_n, subs) + piece, jnp.float32),
                dma((slices,)), dma((slices,)),
                dma((lo_n, slices)), dma((lo_n, slices)), dma((cols_n, slices)),
                dma((units,)), dma((units,)), dma((units,)), dma((units,)), dma((units,)),
                dma((z_n, subs)),
            ],
            compiler_params=pltpu.CompilerParams(
                collective_id=0, has_side_effects=True, vmem_limit_bytes=62 * 1024 * 1024
            ),
            cost_estimate=pl.CostEstimate(flops=flops, bytes_accessed=4 * rows * block, transcendentals=0),
        )(snapshots, mass[:, None])

    in_specs = (P("row", "col"), P("row"))
    return jax.shard_map(shards, mesh=mesh, in_specs=in_specs, out_specs=P("col", "row"), check_vma=False)
```

```python
import functools

import jax
import jax.numpy as jnp
from jax import lax
from jax.experimental import pallas as pl
from jax.experimental.pallas import tpu as pltpu
from jax.sharding import PartitionSpec as P

MESH = pl.DeviceIdType.MESH
LANES = 128
EXTRA = 8


def halves(value):
    high = value.astype(jnp.bfloat16)
    low = (value - high.astype(jnp.float32)).astype(jnp.bfloat16)
    return high, low


def product(left_high, left_low, right_high, right_low):
    dot = functools.partial(jnp.dot, preferred_element_type=jnp.float32)
    return dot(left_high, right_high) + (dot(left_high, right_low) + dot(left_low, right_high))


def kernel(
    rows_n, cols_n, s_ref, mass_ref, out_ref,
    rhs, lhs_high, lhs_low, kept, given, taken, swapped, landed,
    load_sem, y_send, y_recv, own_send, fwd_send, x_recv,
    core_send, core_recv, swap_send, swap_recv, z_send, z_recv,
):
    row, col = lax.axis_index("row"), lax.axis_index("col")
    lo_n, z_n = cols_n // 2, rows_n // 2
    core, z = lax.rem(row, 2), row // 2
    hi, lo = col // lo_n, lax.rem(col, lo_n)
    depth, block = s_ref.shape[0] // 2, s_ref.shape[1]
    slices = block // LANES
    width = out_ref.shape[1]
    subs = width // LANES
    per_block = block // (2 * LANES)
    units = per_block * cols_n
    z_per_block = per_block // subs

    sibling = (row + 1 - 2 * core, col)
    across = (row, (1 - hi) * lo_n + lo)

    def along(d):
        return (row, hi * lo_n + lax.rem(lo + lo_n - d, lo_n))

    def layer(other):
        return (other * 2 + core, col)

    def part(half, sl):
        return s_ref.at[pl.ds(pl.multiple_of(half * depth, depth), depth), pl.ds(sl * LANES, LANES)]

    def copy(src, dst, send, recv, device):
        return pltpu.make_async_remote_copy(
            src_ref=src, dst_ref=dst, send_sem=send, recv_sem=recv, device_id=device, device_id_type=MESH
        )

    def y_copy(sl):
        return copy(part(1 - hi, sl), rhs.at[hi, sl], y_send.at[sl], y_recv.at[sl], across)

    def own_copy(d, sl):
        at = 2 * d + hi
        return copy(part(hi, sl), rhs.at[at, sl], own_send.at[d, sl], x_recv.at[at, sl], along(d))

    def fwd_copy(d, sl):
        at = 2 * d + 1 - hi
        return copy(rhs.at[1 - hi, sl], rhs.at[at, sl], fwd_send.at[d, sl], x_recv.at[at, sl], along(d))

    def core_copy(u):
        return copy(given.at[u], taken.at[u], core_send.at[u], core_recv.at[u], sibling)

    def swap_copy(u):
        return copy(kept.at[u, 1], swapped.at[u], swap_send.at[u], swap_recv.at[u], across)

    def place(u):
        t, rest = u // cols_n, lax.rem(u, cols_n)
        d, e = rest // 2, lax.rem(rest, 2)
        which = lax.rem(e + z, 2)
        at = 2 * d + which
        col_block = which * lo_n + lax.rem(lo + d, lo_n)
        target = col_block * z_per_block + t // subs
        return t, d, at, target, lax.rem(t, subs)

    def slice_of(k, t):
        return (2 * (t // subs) + k) * subs + t % subs

    def z_copy(u):
        _, _, _, target, sub = place(u)
        return copy(kept.at[u, 0], landed.at[z, sub], z_send.at[u], z_recv.at[z, sub], layer(target))

    peers = [sibling, across] + [along(d) for d in range(1, lo_n)]
    peers += [layer(lax.rem(z + d, z_n)) for d in range(1, z_n)]
    barrier = pltpu.get_barrier_semaphore()
    for peer in peers:
        pl.semaphore_signal(barrier, inc=1, device_id=peer, device_id_type=MESH)
    pl.semaphore_wait(barrier, len(peers))

    def load(sl):
        return pltpu.make_async_copy(part(hi, sl), rhs.at[hi, sl], load_sem.at[sl])

    order = [slice_of(k, t) for t in range(per_block) for k in range(2)]
    ahead = 2
    for sl in order[:ahead]:
        y_copy(sl).start()
        for d in range(1, lo_n):
            own_copy(d, sl).start()
    for sl in order:
        load(sl).start()

    mass = mass_ref[:, pl.ds(pl.multiple_of(hi * depth, depth), depth)]
    summed = jnp.broadcast_to(jnp.sum(mass, axis=1, keepdims=True), (EXTRA, LANES))

    def put_left(first, sl, value):
        high, low = halves(jnp.transpose(value) * mass)
        at = pl.ds(first + sl * LANES, LANES)
        lhs_high[at, :] = high
        lhs_low[at, :] = low

    for sl in order:
        load(sl).wait()
        put_left(0, sl, rhs[hi, sl])
    for n, sl in enumerate(order):
        y_copy(sl).wait_send()
        if n + ahead < slices:
            y_copy(order[n + ahead]).start()
        y_copy(sl).wait_recv()
        for d in range(1, lo_n):
            if n >= ahead:
                own_copy(d, sl).start()
            fwd_copy(d, sl).start()
        put_left(block, sl, rhs[1 - hi, sl])

    def compute(u):
        t, d, at, _, _ = place(u)
        mine, theirs = slice_of(core, t), slice_of(1 - core, t)

        @pl.when(d > 0)
        def _():
            for sl in (mine, theirs):
                copy(rhs.at[at, sl], rhs.at[at, sl], own_send.at[0, 0], x_recv.at[at, sl], along(1)).wait_recv()

        right = jnp.concatenate([rhs[at, mine], rhs[at, theirs]], axis=1)
        high, low = halves(right)
        for side in range(2):
            at_rows = pl.ds(side * block, block)
            value = product(lhs_high[at_rows, :], lhs_low[at_rows, :], high, low)
            kept[u, side, :block, :] = value[:, :LANES]
            given[u, side, :block, :] = value[:, LANES:]
            kept[u, side, block:, :] = summed
            given[u, side, block:, :] = summed
        core_copy(u).start()

    def join_cores(u):
        core_copy(u).wait_recv()
        kept[u, 1] = kept[u, 1] + taken[u, 1]
        swap_copy(u).start()
        kept[u, 0] = kept[u, 0] + taken[u, 0]

    def join_across(u):
        _, _, _, target, sub = place(u)
        swap_copy(u).wait_recv()
        value = kept[u, 0] + swapped[u]

        @pl.when(target == z)
        def _():
            landed[z, sub] = value

        @pl.when(target != z)
        def _():
            kept[u, 0] = value
            z_copy(u).start()

    def step(i, carry):
        @pl.when(i >= 2)
        def _():
            join_across(i - 2)

        @pl.when(i < units)
        def _():
            compute(i)
            join_cores(i)

        return carry

    lax.fori_loop(0, units + 2, step, 0)

    for d in range(1, z_n):
        source = lax.rem(z + d, z_n)
        for sub in range(subs):
            copy(
                landed.at[source, sub], landed.at[source, sub], z_send.at[0], z_recv.at[source, sub], layer(source)
            ).wait_recv()
    for sub in range(subs):
        value = landed[0, sub]
        for source in range(1, z_n):
            value = value + landed[source, sub]
        out_ref[:, sub * LANES : (sub + 1) * LANES] = value[:block] / value[block : block + 1]

    for sl in range(slices):
        for d in range(1, lo_n):
            own_copy(d, sl).wait_send()
            fwd_copy(d, sl).wait_send()

    def drain(u, carry):
        core_copy(u).wait_send()
        swap_copy(u).wait_send()

        @pl.when(place(u)[3] != z)
        def _():
            z_copy(u).wait_send()

        return carry

    lax.fori_loop(0, units, drain, 0)


def solution(mesh):
    rows_n, cols_n = mesh.shape["row"], mesh.shape["col"]

    def shards(snapshots, mass):
        rows, block = snapshots.shape
        depth, slices, lo_n, z_n = rows // 2, block // LANES, cols_n // 2, rows_n // 2
        width = block * cols_n // rows_n
        subs = width // LANES
        units = block // (2 * LANES) * cols_n
        piece = (block + EXTRA, LANES)
        dma = pltpu.SemaphoreType.DMA
        flops = 2 * depth * 2 * block * block * cols_n * 3
        return pl.pallas_call(
            functools.partial(kernel, rows_n, cols_n),
            out_shape=jax.ShapeDtypeStruct((block, width), jnp.float32),
            in_specs=[pl.BlockSpec(memory_space=pl.ANY), pl.BlockSpec(memory_space=pltpu.VMEM)],
            out_specs=pl.BlockSpec(memory_space=pltpu.VMEM),
            scratch_shapes=[
                pltpu.VMEM((cols_n, slices, depth, LANES), jnp.float32),
                pltpu.VMEM((2 * block, depth), jnp.bfloat16),
                pltpu.VMEM((2 * block, depth), jnp.bfloat16),
                pltpu.VMEM((units, 2) + piece, jnp.float32),
                pltpu.VMEM((units, 2) + piece, jnp.float32),
                pltpu.VMEM((units, 2) + piece, jnp.float32),
                pltpu.VMEM((units,) + piece, jnp.float32),
                pltpu.VMEM((z_n, subs) + piece, jnp.float32),
                dma((slices,)), dma((slices,)), dma((slices,)),
                dma((lo_n, slices)), dma((lo_n, slices)), dma((cols_n, slices)),
                dma((units,)), dma((units,)), dma((units,)), dma((units,)), dma((units,)),
                dma((z_n, subs)),
            ],
            compiler_params=pltpu.CompilerParams(
                collective_id=0, has_side_effects=True, vmem_limit_bytes=62 * 1024 * 1024
            ),
            cost_estimate=pl.CostEstimate(flops=flops, bytes_accessed=4 * rows * block, transcendentals=0),
        )(snapshots, mass[None, :])

    in_specs = (P("row", "col"), P("row"))
    return jax.shard_map(shards, mesh=mesh, in_specs=in_specs, out_specs=P("col", "row"), check_vma=False)
```

```python
import functools

import jax
import jax.numpy as jnp
from jax import lax
from jax.experimental import pallas as pl
from jax.experimental.pallas import tpu as pltpu
from jax.sharding import PartitionSpec as P

MESH = pl.DeviceIdType.MESH
LANES = 128
EXTRA = 8
SPLIT = 2
LATER = 2


def halves(value):
    high = value.astype(jnp.bfloat16)
    low = (value - high.astype(jnp.float32)).astype(jnp.bfloat16)
    return high, low


def product(left_high, left_low, right_high, right_low):
    dot = functools.partial(jnp.dot, preferred_element_type=jnp.float32)
    return dot(left_high, right_high) + (dot(left_high, right_low) + dot(left_low, right_high))


def kernel(
    rows_n, cols_n, s_ref, mass_ref, out_ref,
    rhs, lhs_high, lhs_low, kept, given, taken, swapped, landed,
    load_sem, y_send, y_recv, own_send, fwd_send, x_recv,
    core_send, core_recv, swap_send, swap_recv, z_send, z_recv,
):
    row, col = lax.axis_index("row"), lax.axis_index("col")
    lo_n, z_n = cols_n // 2, rows_n // 2
    core, z = lax.rem(row, 2), row // 2
    hi, lo = col // lo_n, lax.rem(col, lo_n)
    depth, block = s_ref.shape[0] // 2, s_ref.shape[1]
    slices = block // LANES
    width = out_ref.shape[1]
    subs = width // LANES
    per_block = block // (2 * LANES)
    units = per_block * cols_n
    z_per_block = per_block // subs

    first = lax.rem(1 + z // 2, 2)

    sibling = (row + 1 - 2 * core, col)
    across = (row, (1 - hi) * lo_n + lo)

    def along(d):
        return (row, hi * lo_n + lax.rem(lo + lo_n - d, lo_n))

    def layer(other):
        return (other * 2 + core, col)

    def part(half, sl):
        return s_ref.at[pl.ds(pl.multiple_of(half * depth, depth), depth), pl.ds(sl * LANES, LANES)]

    def copy(src, dst, send, recv, device):
        return pltpu.make_async_remote_copy(
            src_ref=src, dst_ref=dst, send_sem=send, recv_sem=recv, device_id=device, device_id_type=MESH
        )

    def y_copy(sl):
        return copy(part(1 - hi, sl), rhs.at[hi, sl], y_send.at[sl], y_recv.at[sl], across)

    def own_copy(d, sl):
        at = 2 * d + hi
        return copy(part(hi, sl), rhs.at[at, sl], own_send.at[d, sl], x_recv.at[at, sl], along(d))

    def fwd_copy(d, sl):
        at = 2 * d + 1 - hi
        return copy(rhs.at[1 - hi, sl], rhs.at[at, sl], fwd_send.at[d, sl], x_recv.at[at, sl], along(d))

    edges = [0] + [(block // SPLIT) * (h + 1) for h in range(SPLIT - 1)] + [block + EXTRA]
    spans = [pl.ds(edges[h], edges[h + 1] - edges[h]) for h in range(SPLIT)]

    def core_copy(u, side):
        return copy(given.at[u, side], taken.at[u, side], core_send.at[u, side], core_recv.at[u, side], sibling)

    def swap_copy(u, h):
        return copy(kept.at[u, 1, spans[h]], swapped.at[u, spans[h]], swap_send.at[u, h], swap_recv.at[u, h], across)

    def place(u):
        t, rest = u // cols_n, lax.rem(u, cols_n)
        d, e = rest // 2, lax.rem(rest, 2)
        which = lax.rem(e + first, 2)
        at = 2 * d + which
        col_block = which * lo_n + lax.rem(lo + d, lo_n)
        target = col_block * z_per_block + t // subs
        return t, d, at, target, lax.rem(t, subs)

    def slice_of(k, t):
        return (2 * (t // subs) + k) * subs + t % subs

    def z_copy(u, h):
        _, _, _, target, sub = place(u)
        return copy(
            kept.at[u, 0, spans[h]], landed.at[z, sub, spans[h]], z_send.at[u, h], z_recv.at[z, sub, h], layer(target)
        )

    peers = [sibling, across] + [along(d) for d in range(1, lo_n)]
    peers += [layer(lax.rem(z + d, z_n)) for d in range(1, z_n)]
    barrier = pltpu.get_barrier_semaphore()
    for peer in peers:
        pl.semaphore_signal(barrier, inc=1, device_id=peer, device_id_type=MESH)
    pl.semaphore_wait(barrier, len(peers))

    def load(sl):
        return pltpu.make_async_copy(part(hi, sl), rhs.at[hi, sl], load_sem.at[sl])

    order = [slice_of(k, t) for t in range(per_block) for k in range(2)]
    ahead = 2
    for sl in order[:ahead]:
        y_copy(sl).start()
        for d in range(1, lo_n):
            own_copy(d, sl).start()
    for sl in order:
        load(sl).start()

    mass = mass_ref[:, pl.ds(pl.multiple_of(hi * depth, depth), depth)]
    summed = jnp.broadcast_to(jnp.sum(mass, axis=1, keepdims=True), (EXTRA, LANES))

    def put_left(first, sl, value):
        high, low = halves(jnp.transpose(value) * mass)
        at = pl.ds(first + sl * LANES, LANES)
        lhs_high[at, :] = high
        lhs_low[at, :] = low

    for sl in order:
        load(sl).wait()
        put_left(0, sl, rhs[hi, sl])
    def send_later(sl, own):
        @pl.when(own)
        def _():
            for d in range(1, lo_n):
                own_copy(d, sl).start()

        @pl.when(jnp.logical_not(own))
        def _():
            for d in range(1, lo_n):
                fwd_copy(d, sl).start()

    for n, sl in enumerate(order):
        y_copy(sl).wait_send()
        if n + ahead < slices:
            y_copy(order[n + ahead]).start()
        y_copy(sl).wait_recv()
        if n < ahead:
            for d in range(1, lo_n):
                fwd_copy(d, sl).start()
        else:
            send_later(sl, hi == first)
        put_left(block, sl, rhs[1 - hi, sl])

    def compute(u):
        t, d, at, _, _ = place(u)
        mine, theirs = slice_of(core, t), slice_of(1 - core, t)

        @pl.when(d > 0)
        def _():
            for sl in (mine, theirs):
                copy(rhs.at[at, sl], rhs.at[at, sl], own_send.at[0, 0], x_recv.at[at, sl], along(1)).wait_recv()

        right = jnp.concatenate([rhs[at, mine], rhs[at, theirs]], axis=1)
        high, low = halves(right)
        for side in (1, 0):
            at_rows = pl.ds(side * block, block)
            value = product(lhs_high[at_rows, :], lhs_low[at_rows, :], high, low)
            kept[u, side, :block, :] = value[:, :LANES]
            given[u, side, :block, :] = value[:, LANES:]
            kept[u, side, block:, :] = summed
            given[u, side, block:, :] = summed
            core_copy(u, side).start()

    def join_cores(u):
        core_copy(u, 1).wait_recv()
        for h in range(SPLIT):
            kept[u, 1, spans[h]] = kept[u, 1, spans[h]] + taken[u, 1, spans[h]]
            swap_copy(u, h).start()
        core_copy(u, 0).wait_recv()
        kept[u, 0] = kept[u, 0] + taken[u, 0]

    def join_across(u):
        _, _, _, target, sub = place(u)
        for h in range(SPLIT):
            swap_copy(u, h).wait_recv()
            value = kept[u, 0, spans[h]] + swapped[u, spans[h]]

            @pl.when(target == z)
            def _():
                landed[z, sub, spans[h]] = value

            @pl.when(target != z)
            def _():
                kept[u, 0, spans[h]] = value
                z_copy(u, h).start()

    def step(i, carry):
        @pl.when(i == LATER)
        def _():
            for sl in order[ahead:]:
                send_later(sl, hi != first)

        @pl.when(i >= 2)
        def _():
            join_across(i - 2)

        @pl.when(i < units)
        def _():
            compute(i)
            join_cores(i)

        return carry

    lax.fori_loop(0, units + 2, step, 0)

    for d in range(1, z_n):
        source = lax.rem(z + d, z_n)
        for sub in range(subs):
            for h in range(SPLIT):
                piece = landed.at[source, sub, spans[h]]
                copy(piece, piece, z_send.at[0, 0], z_recv.at[source, sub, h], layer(source)).wait_recv()
    for sub in range(subs):
        value = landed[0, sub]
        for source in range(1, z_n):
            value = value + landed[source, sub]
        out_ref[:, sub * LANES : (sub + 1) * LANES] = value[:block] / value[block : block + 1]

    for sl in range(slices):
        for d in range(1, lo_n):
            own_copy(d, sl).wait_send()
            fwd_copy(d, sl).wait_send()

    def drain(u, carry):
        for side in range(2):
            core_copy(u, side).wait_send()
        for h in range(SPLIT):
            swap_copy(u, h).wait_send()

        @pl.when(place(u)[3] != z)
        def _():
            for h in range(SPLIT):
                z_copy(u, h).wait_send()

        return carry

    lax.fori_loop(0, units, drain, 0)


def solution(mesh):
    rows_n, cols_n = mesh.shape["row"], mesh.shape["col"]

    def shards(snapshots, mass):
        rows, block = snapshots.shape
        depth, slices, lo_n, z_n = rows // 2, block // LANES, cols_n // 2, rows_n // 2
        width = block * cols_n // rows_n
        subs = width // LANES
        units = block // (2 * LANES) * cols_n
        piece = (block + EXTRA, LANES)
        dma = pltpu.SemaphoreType.DMA
        flops = 2 * depth * 2 * block * block * cols_n * 3
        return pl.pallas_call(
            functools.partial(kernel, rows_n, cols_n),
            out_shape=jax.ShapeDtypeStruct((block, width), jnp.float32),
            in_specs=[pl.BlockSpec(memory_space=pl.ANY), pl.BlockSpec(memory_space=pltpu.VMEM)],
            out_specs=pl.BlockSpec(memory_space=pltpu.VMEM),
            scratch_shapes=[
                pltpu.VMEM((cols_n, slices, depth, LANES), jnp.float32),
                pltpu.VMEM((2 * block, depth), jnp.bfloat16),
                pltpu.VMEM((2 * block, depth), jnp.bfloat16),
                pltpu.VMEM((units, 2) + piece, jnp.float32),
                pltpu.VMEM((units, 2) + piece, jnp.float32),
                pltpu.VMEM((units, 2) + piece, jnp.float32),
                pltpu.VMEM((units,) + piece, jnp.float32),
                pltpu.VMEM((z_n, subs) + piece, jnp.float32),
                dma((slices,)), dma((slices,)), dma((slices,)),
                dma((lo_n, slices)), dma((lo_n, slices)), dma((cols_n, slices)),
                dma((units, 2)), dma((units, 2)), dma((units, SPLIT)), dma((units, SPLIT)), dma((units, SPLIT)),
                dma((z_n, subs, SPLIT)),
            ],
            compiler_params=pltpu.CompilerParams(
                collective_id=0, has_side_effects=True, vmem_limit_bytes=62 * 1024 * 1024
            ),
            cost_estimate=pl.CostEstimate(flops=flops, bytes_accessed=4 * rows * block, transcendentals=0),
        )(snapshots, mass[None, :])

    in_specs = (P("row", "col"), P("row"))
    return jax.shard_map(shards, mesh=mesh, in_specs=in_specs, out_specs=P("col", "row"), check_vma=False)
```

```python
import functools

import jax
import jax.numpy as jnp
from jax import lax
from jax.experimental import pallas as pl
from jax.experimental.pallas import tpu as pltpu
from jax.sharding import PartitionSpec as P

MESH = pl.DeviceIdType.MESH
LANES = 128
EXTRA = 8
SPLIT = 2
LATER = 2


def halves(value):
    high = value.astype(jnp.bfloat16)
    low = (value - high.astype(jnp.float32)).astype(jnp.bfloat16)
    return high, low


def product(left_high, left_low, right_high, right_low):
    dot = functools.partial(jnp.dot, preferred_element_type=jnp.float32)
    return dot(left_high, right_high) + (dot(left_high, right_low) + dot(left_low, right_high))


def kernel(
    rows_n, cols_n, s_ref, mass_ref, out_ref,
    rhs, lhs_high, lhs_low, kept, given, taken, swapped, landed,
    load_sem, y_send, y_recv, own_send, fwd_send, x_recv,
    core_send, core_recv, swap_send, swap_recv, z_send, z_recv,
):
    row, col = lax.axis_index("row"), lax.axis_index("col")
    lo_n, z_n = cols_n // 2, rows_n // 2
    core, z = lax.rem(row, 2), row // 2
    hi, lo = col // lo_n, lax.rem(col, lo_n)
    depth, block = s_ref.shape[0] // 2, s_ref.shape[1]
    slices = block // LANES
    width = out_ref.shape[1]
    subs = width // LANES
    per_block = block // (2 * LANES)
    units = per_block * cols_n
    z_per_block = per_block // subs

    first = lax.rem(1 + z // 2, 2)

    sibling = (row + 1 - 2 * core, col)
    across = (row, (1 - hi) * lo_n + lo)

    def along(d):
        return (row, hi * lo_n + lax.rem(lo + lo_n - d, lo_n))

    def layer(other):
        return (other * 2 + core, col)

    def part(half, sl):
        return s_ref.at[pl.ds(pl.multiple_of(half * depth, depth), depth), pl.ds(sl * LANES, LANES)]

    def copy(src, dst, send, recv, device):
        return pltpu.make_async_remote_copy(
            src_ref=src, dst_ref=dst, send_sem=send, recv_sem=recv, device_id=device, device_id_type=MESH
        )

    def y_copy(sl):
        return copy(part(1 - hi, sl), rhs.at[hi, sl], y_send.at[sl], y_recv.at[sl], across)

    def own_copy(d, sl):
        at = 2 * d + hi
        return copy(part(hi, sl), rhs.at[at, sl], own_send.at[d, sl], x_recv.at[at, sl], along(d))

    def fwd_copy(d, sl):
        at = 2 * d + 1 - hi
        return copy(rhs.at[1 - hi, sl], rhs.at[at, sl], fwd_send.at[d, sl], x_recv.at[at, sl], along(d))

    edges = [0] + [(block // SPLIT) * (h + 1) for h in range(SPLIT - 1)] + [block + EXTRA]
    spans = [pl.ds(edges[h], edges[h + 1] - edges[h]) for h in range(SPLIT)]

    def core_copy(u, side):
        return copy(given.at[u, side], taken.at[u, side], core_send.at[u, side], core_recv.at[u, side], sibling)

    def swap_copy(u, h):
        return copy(kept.at[u, 1, spans[h]], swapped.at[u, spans[h]], swap_send.at[u, h], swap_recv.at[u, h], across)

    def place(u):
        t, rest = u // cols_n, lax.rem(u, cols_n)
        d, e = rest // 2, lax.rem(rest, 2)
        which = lax.rem(e + first, 2)
        at = 2 * d + which
        col_block = which * lo_n + lax.rem(lo + d, lo_n)
        target = col_block * z_per_block + t // subs
        return t, d, at, target, lax.rem(t, subs)

    def slice_of(k, t):
        return (2 * (t // subs) + k) * subs + t % subs

    def z_copy(u, h):
        _, _, _, target, sub = place(u)
        return copy(
            kept.at[u, 0, spans[h]], landed.at[z, sub, spans[h]], z_send.at[u, h], z_recv.at[z, sub, h], layer(target)
        )

    peers = [sibling, across] + [along(d) for d in range(1, lo_n)]
    peers += [layer(lax.rem(z + d, z_n)) for d in range(1, z_n)]
    barrier = pltpu.get_barrier_semaphore()
    for peer in peers:
        pl.semaphore_signal(barrier, inc=1, device_id=peer, device_id_type=MESH)
    pl.semaphore_wait(barrier, len(peers))

    def load(sl):
        return pltpu.make_async_copy(part(hi, sl), rhs.at[hi, sl], load_sem.at[sl])

    order = [slice_of(k, t) for t in range(per_block) for k in range(2)]
    ahead = 2
    for sl in order[:ahead]:
        y_copy(sl).start()
        for d in range(1, lo_n):
            own_copy(d, sl).start()
    for sl in order:
        load(sl).start()

    mass = mass_ref[:, pl.ds(pl.multiple_of(hi * depth, depth), depth)]
    summed = jnp.broadcast_to(jnp.sum(mass, axis=1, keepdims=True), (EXTRA, LANES))

    def put_left(first, sl, value):
        high, low = halves(jnp.transpose(value) * mass)
        at = pl.ds(first + sl * LANES, LANES)
        lhs_high[at, :] = high
        lhs_low[at, :] = low

    for sl in order:
        load(sl).wait()
        put_left(0, sl, rhs[hi, sl])
    def send_later(sl, own):
        @pl.when(own)
        def _():
            for d in range(1, lo_n):
                own_copy(d, sl).start()

        @pl.when(jnp.logical_not(own))
        def _():
            for d in range(1, lo_n):
                fwd_copy(d, sl).start()

    for n, sl in enumerate(order):
        y_copy(sl).wait_send()
        if n + ahead < slices:
            y_copy(order[n + ahead]).start()
        y_copy(sl).wait_recv()
        if n < ahead:
            for d in range(1, lo_n):
                fwd_copy(d, sl).start()
        else:
            send_later(sl, hi == first)
        put_left(block, sl, rhs[1 - hi, sl])

    def compute(u):
        t, d, at, _, _ = place(u)
        mine, theirs = slice_of(core, t), slice_of(1 - core, t)

        @pl.when(d > 0)
        def _():
            for sl in (mine, theirs):
                copy(rhs.at[at, sl], rhs.at[at, sl], own_send.at[0, 0], x_recv.at[at, sl], along(1)).wait_recv()

        right = jnp.concatenate([rhs[at, mine], rhs[at, theirs]], axis=1)
        high, low = halves(right)
        for side in (1, 0):
            at_rows = pl.ds(side * block, block)
            value = product(lhs_high[at_rows, :], lhs_low[at_rows, :], high, low)
            kept[u, side, :block, :] = value[:, :LANES]
            given[u, side, :block, :] = value[:, LANES:]
            kept[u, side, block:, :] = summed
            given[u, side, block:, :] = summed
            core_copy(u, side).start()

    def join_cores(u):
        core_copy(u, 1).wait_recv()
        for h in range(SPLIT):
            kept[u, 1, spans[h]] = kept[u, 1, spans[h]] + taken[u, 1, spans[h]]
            swap_copy(u, h).start()
        core_copy(u, 0).wait_recv()
        kept[u, 0] = kept[u, 0] + taken[u, 0]

    def join_across(u):
        _, _, _, target, sub = place(u)
        for h in range(SPLIT):
            swap_copy(u, h).wait_recv()
            value = kept[u, 0, spans[h]] + swapped[u, spans[h]]

            @pl.when(target == z)
            def _():
                landed[z, sub, spans[h]] = value

            @pl.when(target != z)
            def _():
                kept[u, 0, spans[h]] = value
                z_copy(u, h).start()

    def step(i, carry):
        @pl.when(i == LATER)
        def _():
            for sl in order[ahead:]:
                send_later(sl, hi != first)

        @pl.when(i < units)
        def _():
            compute(i)
            join_cores(i)

        @pl.when(i >= 2)
        def _():
            join_across(i - 2)

        return carry

    lax.fori_loop(0, units + 2, step, 0)

    for d in range(1, z_n):
        source = lax.rem(z + d, z_n)
        for sub in range(subs):
            for h in range(SPLIT):
                piece = landed.at[source, sub, spans[h]]
                copy(piece, piece, z_send.at[0, 0], z_recv.at[source, sub, h], layer(source)).wait_recv()
    for sub in range(subs):
        value = landed[0, sub]
        for source in range(1, z_n):
            value = value + landed[source, sub]
        out_ref[:, sub * LANES : (sub + 1) * LANES] = value[:block] / value[block : block + 1]

    for sl in range(slices):
        for d in range(1, lo_n):
            own_copy(d, sl).wait_send()
            fwd_copy(d, sl).wait_send()

    def drain(u, carry):
        for side in range(2):
            core_copy(u, side).wait_send()
        for h in range(SPLIT):
            swap_copy(u, h).wait_send()

        @pl.when(place(u)[3] != z)
        def _():
            for h in range(SPLIT):
                z_copy(u, h).wait_send()

        return carry

    lax.fori_loop(0, units, drain, 0)


def solution(mesh):
    rows_n, cols_n = mesh.shape["row"], mesh.shape["col"]

    def shards(snapshots, mass):
        rows, block = snapshots.shape
        depth, slices, lo_n, z_n = rows // 2, block // LANES, cols_n // 2, rows_n // 2
        width = block * cols_n // rows_n
        subs = width // LANES
        units = block // (2 * LANES) * cols_n
        piece = (block + EXTRA, LANES)
        dma = pltpu.SemaphoreType.DMA
        flops = 2 * depth * 2 * block * block * cols_n * 3
        return pl.pallas_call(
            functools.partial(kernel, rows_n, cols_n),
            out_shape=jax.ShapeDtypeStruct((block, width), jnp.float32),
            in_specs=[pl.BlockSpec(memory_space=pl.ANY), pl.BlockSpec(memory_space=pltpu.VMEM)],
            out_specs=pl.BlockSpec(memory_space=pltpu.VMEM),
            scratch_shapes=[
                pltpu.VMEM((cols_n, slices, depth, LANES), jnp.float32),
                pltpu.VMEM((2 * block, depth), jnp.bfloat16),
                pltpu.VMEM((2 * block, depth), jnp.bfloat16),
                pltpu.VMEM((units, 2) + piece, jnp.float32),
                pltpu.VMEM((units, 2) + piece, jnp.float32),
                pltpu.VMEM((units, 2) + piece, jnp.float32),
                pltpu.VMEM((units,) + piece, jnp.float32),
                pltpu.VMEM((z_n, subs) + piece, jnp.float32),
                dma((slices,)), dma((slices,)), dma((slices,)),
                dma((lo_n, slices)), dma((lo_n, slices)), dma((cols_n, slices)),
                dma((units, 2)), dma((units, 2)), dma((units, SPLIT)), dma((units, SPLIT)), dma((units, SPLIT)),
                dma((z_n, subs, SPLIT)),
            ],
            compiler_params=pltpu.CompilerParams(
                collective_id=0, has_side_effects=True, vmem_limit_bytes=62 * 1024 * 1024
            ),
            cost_estimate=pl.CostEstimate(flops=flops, bytes_accessed=4 * rows * block, transcendentals=0),
        )(snapshots, mass[None, :])

    in_specs = (P("row", "col"), P("row"))
    return jax.shard_map(shards, mesh=mesh, in_specs=in_specs, out_specs=P("col", "row"), check_vma=False)
```
